512 devices in a mesh: dp: 16 (over x, z_hi, core), mp: 32 (over z_lo, y).
Axes of the slice: x: 4, y: 4, z: 16 (z_hi: 2, z_lo: 8; z = z_hi * 8 + z_lo), core: 2. Of those that a mesh axis runs over, the one named last changes fastest.
Arguments:
- patches: bfloat16 [8192, 3072], P(('dp', 'mp')), may hold values from -24 to 24
- qkv_weight: bfloat16 [3072, 12288], P(None, 'mp'), may hold values from -1 to 1
- context_grad: bfloat16 [8192, 4096], P('dp', 'mp'), may hold values from -6 to 6
Outputs:
- patch_grad: bfloat16 [8192, 3072], P(('dp', 'mp'))
- weight_grad: bfloat16 [3072, 12288], P(None, 'mp')
The draws below stay inside these ranges and needn't reach their ends.
All inputs are finite; a program needn't handle non-finite values.
Results may differ from the reference program's by a relative error of at most 0.03.
Values may be sent and summed in bfloat16 or wider, within the bound.
A program may use at most 64 MiB of HBM per device.

```python
import math
import jax
import jax.numpy as jnp
from jax import lax

D = 3072
HD = 128
PATCHES = 256
IMAGES_DEV = 2
HEADS = 32
TOKENS = 8192
QKV = 12288
N_DP = 16


def draw_patches(key, part):
    key = jax.random.fold_in(key, 11)
    key_rows, key_base = jax.random.split(key, 2)
    scales = jnp.exp(jax.random.uniform(key_rows, (TOKENS, 1), jnp.float32, math.log(0.5), math.log(5.0)))
    values = jax.random.normal(key_base, (TOKENS, D), jnp.float32) * scales
    return jnp.clip(values, -24.0, 24.0).astype(jnp.bfloat16)


def draw_qkv_weight(key, part):
    key = jax.random.fold_in(key, 23)
    key_cols, key_base = jax.random.split(key, 2)
    scales = jnp.exp(jax.random.uniform(key_cols, (1, QKV), jnp.float32, 0.0, math.log(10.0)))
    base = jax.random.normal(key_base, (D, QKV), jnp.float32)
    values = base * scales * (1.0 / math.sqrt(D))
    return jnp.clip(values, -1.0, 1.0).astype(jnp.bfloat16)


def block_scale(key, shape, pieces, smallest, top_value):
    loudness = 1.0
    for axis_at, shards_of in pieces:
        draws = jax.random.uniform(jax.random.fold_in(jax.random.fold_in(key, 6), axis_at), (shards_of,), jnp.float32, smallest / len(pieces), top_value / len(pieces))
        loudness = loudness * jnp.repeat(jnp.exp(draws), shape[axis_at] // shards_of).reshape((-1,) + (1,) * (len(shape) - 1 - axis_at))
    return loudness


def scatter_about(rng, shape, deviation, most, pieces=(), held_as=jnp.bfloat16):
    entries = deviation * jax.random.normal(rng, shape, jnp.float32)
    if pieces:
        entries = entries * block_scale(rng, shape, pieces, -0.22, 0.18)
    return jnp.clip(entries, -most, most).astype(held_as)


def setup_inputs(seed: int = 0) -> dict:
    seeds = jax.random.split(jax.random.key(seed), 4)
    patches = draw_patches(jax.random.fold_in(seeds[3], 71), 0)
    qkv_weight = draw_qkv_weight(jax.random.fold_in(seeds[3], 71), 0)
    context_grad = scatter_about(seeds[2], (TOKENS, HEADS * HD), 1.0, 6.0, ((0, 16), (1, 32)))
    return dict(patches=patches, qkv_weight=qkv_weight, context_grad=context_grad)


def layer_normalize(values):
    centred = values - lax.optimization_barrier(jnp.mean(values, axis=-1, keepdims=True))
    variance = lax.optimization_barrier(jnp.mean(centred * centred, axis=-1, keepdims=True))
    rscale = lax.rsqrt(variance + 1e-06)
    return (centred * rscale, rscale)

def norm_backward(grads, normed, rscale):
    return (grads - lax.optimization_barrier(jnp.mean(grads, axis=-1, keepdims=True)) - normed * lax.optimization_barrier(jnp.mean(grads * normed, axis=-1, keepdims=True))) * rscale

def attention_back(qkv, context):
    rows_n = qkv.shape[0]
    heads = qkv.shape[1] // (3 * HD)
    split = qkv.reshape(rows_n, heads, 3, HD)
    query = split[:, :, 0, :].astype(jnp.float32)
    key_tensor = split[:, :, 1, :].astype(jnp.float32)
    values = split[:, :, 2, :]
    context = context.reshape(rows_n, heads, HD)
    qnorm, qscale = layer_normalize(query)
    normed_keys, key_scale = layer_normalize(key_tensor)
    rounded_queries = qnorm.astype(jnp.bfloat16)
    rounded_keys = normed_keys.astype(jnp.bfloat16)
    score_factor = 1.0 / HD ** 0.5
    logit_scores = jnp.einsum('wqg,zqg->qwz', rounded_queries.astype(jnp.float32), rounded_keys.astype(jnp.float32)) * score_factor
    expo = jnp.exp(logit_scores)
    probs = expo / lax.optimization_barrier(jnp.sum(expo, axis=-1, keepdims=True))
    pround = probs.astype(jnp.bfloat16)
    dsoft = jnp.einsum('wqg,zqg->qwz', context.astype(jnp.float32), values.astype(jnp.float32))
    delta = lax.optimization_barrier(jnp.sum(probs * dsoft, axis=-1, keepdims=True))
    score_grad = (probs * (dsoft - delta) * score_factor).astype(jnp.bfloat16)
    dvalue = jnp.einsum('hpj,phd->jhd', pround.astype(jnp.float32), context.astype(jnp.float32))
    normed_query_grad = jnp.einsum('rcw,wrt->crt', score_grad.astype(jnp.float32), rounded_keys.astype(jnp.float32))
    normed_key_grad = jnp.einsum('hpj,phd->jhd', score_grad.astype(jnp.float32), rounded_queries.astype(jnp.float32))
    dquery = norm_backward(normed_query_grad, qnorm, qscale)
    key_cotangent = norm_backward(normed_key_grad, normed_keys, key_scale)
    joined = jnp.stack([dquery, key_cotangent, dvalue], axis=2)
    return joined.astype(jnp.bfloat16).reshape(rows_n, heads * 3 * HD)

def reference(patches, qkv_weight, context_grad):
    heads = qkv_weight.shape[1] // (3 * HD)
    weight_full = qkv_weight.astype(jnp.float32).reshape(D, heads, 3 * HD)
    images = patches.reshape(N_DP * IMAGES_DEV, PATCHES, D)
    contexts = context_grad.reshape(N_DP * IMAGES_DEV, PATCHES, heads * HD)

    def one_image(carry, pair):
        image, context = pair
        qkv = jnp.dot(image, qkv_weight, preferred_element_type=jnp.float32).astype(jnp.bfloat16)
        qkv_grad = attention_back(qkv, context)
        per_head = jnp.einsum('phc,dhc->hpd', qkv_grad.astype(jnp.float32).reshape(PATCHES, heads, 3 * HD), weight_full)
        rounded = lax.optimization_barrier(per_head.astype(jnp.bfloat16)).astype(jnp.float32)
        image_grad = lax.optimization_barrier(jnp.sum(rounded, axis=0)).astype(jnp.bfloat16)
        return (carry, (image_grad, qkv_grad))
    unused, (grads, qkv_grads) = lax.scan(one_image, jnp.zeros((), jnp.float32), (images, contexts))
    group_rows = patches.reshape(N_DP, IMAGES_DEV * PATCHES, D)
    group_grads = qkv_grads.reshape(N_DP, IMAGES_DEV * PATCHES, heads * 3 * HD)

    def one_group(carry, pair):
        rows, grad_rows = pair
        term = jnp.dot(rows.T, grad_rows, preferred_element_type=jnp.float32)
        term = lax.optimization_barrier(term.astype(jnp.bfloat16)).astype(jnp.float32)
        return (carry + term, jnp.zeros((), jnp.float32))
    start = jnp.zeros((D, heads * 3 * HD), jnp.float32)
    total, unused_two = lax.scan(one_group, start, (group_rows, group_grads))
    return (grads.reshape(N_DP * IMAGES_DEV * PATCHES, D), total.astype(jnp.bfloat16))
```

```python
import functools
import jax
import jax.numpy as jnp
from jax import lax
from jax.experimental import pallas as pl
from jax.experimental.pallas import tpu as pltpu
from jax.sharding import PartitionSpec as P

MESH = pl.DeviceIdType.MESH
NZ, NY, NX = 8, 4, 4
HD = 128
PATCHES = 256
F32, BF16 = jnp.float32, jnp.bfloat16


def when(cond, fn):
    pl.when(cond)(fn)

def ag_kernel(S, x_ref, g_ref, zs, zr, ys, yr, lsem):
    dp = lax.axis_index("dp"); mp = lax.axis_index("mp")
    z = mp // NY; y = lax.rem(mp, NY)
    yp = lax.rem(y + 1, NY); ym = lax.rem(y + NY - 1, NY)
    half = x_ref.shape[1] // 2
    def zdev(t): return (dp, t * NY + y)
    def ydev(t): return (dp, z * NY + t)
    def ok(t): return jnp.logical_and(t >= 0, t < NZ)
    bar = pltpu.get_barrier_semaphore()
    cnt = jnp.int32(2)
    pl.semaphore_signal(bar, inc=1, device_id=ydev(yp), device_id_type=MESH)
    pl.semaphore_signal(bar, inc=1, device_id=ydev(ym), device_id_type=MESH)
    for s in range(1, S + 1):
        for sg in (-1, 1):
            t = z + sg * s
            when(ok(t), lambda t=t: pl.semaphore_signal(bar, inc=1, device_id=zdev(t), device_id_type=MESH))
            cnt = cnt + ok(t).astype(jnp.int32)
    own = pltpu.make_async_copy(x_ref, g_ref.at[mp], lsem)
    own.start()
    pl.semaphore_wait(bar, cnt)
    own.wait()

    def zcopy(j, t, k):
        b = g_ref.at[j * NY + y]
        return pltpu.make_async_remote_copy(b, b, zs.at[j, k], zr.at[j], device_id=zdev(t), device_id_type=MESH)
    def ycopy(j, k):
        if k < 2:
            b = g_ref.at[j * NY + y]
        elif k == 2:
            b = g_ref.at[j * NY + ym, :, pl.ds(0, half)]
        else:
            b = g_ref.at[j * NY + yp, :, pl.ds(half, half)]
        return pltpu.make_async_remote_copy(b, b, ys.at[j, k], yr.at[j, k], device_id=ydev(yp if k % 2 == 0 else ym), device_id_type=MESH)
    def yarrive(j, k):
        yy = lax.rem(y + (3, 1, 2, 2)[k], NY)
        b = g_ref.at[j * NY + yy]
        if k == 2: b = g_ref.at[j * NY + yy, :, pl.ds(0, half)]
        if k == 3: b = g_ref.at[j * NY + yy, :, pl.ds(half, half)]
        return pltpu.make_async_remote_copy(b, b, ys.at[j, k], yr.at[j, k], device_id=ydev(yp), device_id_type=MESH)
    def forward(j):
        yarrive(j, 0).wait_recv(); ycopy(j, 2).start()
        yarrive(j, 1).wait_recv(); ycopy(j, 3).start()

    for s in range(1, S + 1):
        for i, sg in enumerate((-1, 1)):
            t = z + sg * s
            when(ok(t), lambda t=t, k=2 * (s - 1) + i: zcopy(z, t, k).start())
    ycopy(z, 0).start(); ycopy(z, 1).start()
    for d in range(1, NZ):
        for i, sg in enumerate((-1, 1)):
            j = z + sg * d
            def take(j=j, sg=sg, d=d):
                zcopy(j, z, 0).wait_recv()
                if d % S == 0:
                    for s in range(1, S + 1):
                        t = z - sg * s
                        when(ok(t), lambda t=t, s=s: zcopy(j, t, s - 1).start())
                ycopy(j, 0).start(); ycopy(j, 1).start()
            when(ok(j), take)
        if d == 1:
            forward(z)
        else:
            for sg in (-1, 1):
                j = z + sg * (d - 1)
                when(ok(j), functools.partial(forward, j))
    for sg in (-1, 1):
        j = z + sg * (NZ - 1)
        when(ok(j), functools.partial(forward, j))
    for j in range(NZ):
        yarrive(j, 2).wait_recv(); yarrive(j, 3).wait_recv()
        for k in range(4):
            ycopy(j, k).wait_send()
    for s in range(1, S + 1):
        for i, sg in enumerate((-1, 1)):
            t = z + sg * s
            when(ok(t), lambda t=t, k=2 * (s - 1) + i: zcopy(z, t, k).wait_send())
    for d in range(S, NZ, S):
        for sg in (-1, 1):
            j = z + sg * d
            for s in range(1, S + 1):
                t = z - sg * s
                when(jnp.logical_and(ok(j), ok(t)), lambda j=j, t=t, s=s: zcopy(j, t, s - 1).wait_send())

def gather_patches(x, S, cid=0, name="gather_patches"):
    return pl.pallas_call(
        functools.partial(ag_kernel, S),
        out_shape=jax.ShapeDtypeStruct((NZ * NY, *x.shape), x.dtype),
        in_specs=[pl.BlockSpec(memory_space=pltpu.VMEM)],
        out_specs=pl.BlockSpec(memory_space=pltpu.VMEM),
        scratch_shapes=[pltpu.SemaphoreType.DMA((NZ, 2 * S)), pltpu.SemaphoreType.DMA((NZ,)),
                        pltpu.SemaphoreType.DMA((NZ, 4)), pltpu.SemaphoreType.DMA((NZ, 4)), pltpu.SemaphoreType.DMA],
        compiler_params=pltpu.CompilerParams(collective_id=cid, has_side_effects=True, vmem_limit_bytes=48 << 20),
        name=name,
    )(x)


def add(*terms):
    total = terms[0].astype(F32)
    for t in terms[1:]:
        total = total + t.astype(F32)
    return total.astype(BF16)

def far_first(i, z):
    right = z >= NZ // 2
    near = jnp.where(right, z, NZ - 1 - z)
    alone = 2 * near - (NZ - 1)
    over = jnp.maximum(i - alone, 0)
    d = (NZ - 1 - near) - over // 2
    j = jnp.where(i < alone, i, jnp.where(over % 2 == 0, near - d, near + d))
    return jnp.where(right, j, NZ - 1 - j)

def reduce_kernel(Q, R, pt, wt, pg, wg,
                  bufa, sendb, recvb, sendc, recvc,
                  y1, sendy, recvy, colsum, zin, zin2,
                  sa, ra, sb, rb, sc, rc, sd, rd, se, re, s1, r1, s2, r2, szs, szr):
    dp = lax.axis_index("dp"); mp = lax.axis_index("mp")
    x = dp // 4; zh = lax.rem(dp // 2, 2); c = lax.rem(dp, 2)
    z = mp // NY; y = lax.rem(mp, NY)
    yp = lax.rem(y + 1, NY); ym = lax.rem(y + NY - 1, NY); y2 = lax.rem(y + 2, NY)
    width = pt.shape[2]; half = width // 2
    lo, hi = pl.ds(0, half), pl.ds(half, half)
    sib = (x * 4 + zh * 2 + (1 - c), mp)
    far = (x * 4 + (1 - zh) * 2 + c, mp)
    def xdev(k): return (lax.rem(x + k, NX) * 4 + zh * 2 + c, mp)
    def ydev(t): return (dp, z * NY + t)
    def zdev(t): return (dp, t * NY + y)
    def remote(src, dst, ss, rs, dev):
        return pltpu.make_async_remote_copy(src, dst, ss, rs, device_id=dev, device_id_type=MESH)

    bar = pltpu.get_barrier_semaphore()
    has_l, has_r = z > 0, z < NZ - 1
    for dev in (sib, far, xdev(1), xdev(2), xdev(3), ydev(yp), ydev(ym)):
        pl.semaphore_signal(bar, inc=1, device_id=dev, device_id_type=MESH)
    when(has_l, lambda: pl.semaphore_signal(bar, inc=1, device_id=zdev(z - 1), device_id_type=MESH))
    when(has_r, lambda: pl.semaphore_signal(bar, inc=1, device_id=zdev(z + 1), device_id_type=MESH))
    pl.semaphore_wait(bar, 7 + has_l.astype(jnp.int32) + has_r.astype(jnp.int32))

    def cp_a(q): return remote(wt.at[1 - c, q], bufa.at[q], sa.at[q], ra.at[q], sib)
    def cp_b(q, k): return remote(sendb.at[q, k - 1], recvb.at[q, k - 1], sb.at[q, k - 1], rb.at[q, k - 1], xdev(k))
    def cp_c(q): return remote(sendc.at[q], recvc.at[q], sc.at[q], rc.at[q], far)
    def cp_d(q, k):
        b = wg.at[c, q, x]
        return remote(b, b, sd.at[q, k], rd.at[q, k], sib if k == 0 else xdev(k))
    def arr_d(q, k):
        b = wg.at[1 - c, q, x] if k == 0 else wg.at[c, q, lax.rem(x + NX - k, NX)]
        return remote(b, b, sd.at[q, k], rd.at[q, k], sib)
    def cp_e(q, k):
        b = wg.at[c, q, lax.rem(x + NX - k, NX)]
        return remote(b, b, se.at[q, k - 1], re.at[q, k - 1], sib)
    def arr_e(q, k):
        b = wg.at[1 - c, q, lax.rem(x + NX - k, NX)]
        return remote(b, b, se.at[q, k - 1], re.at[q, k - 1], sib)
    def stage_b(q):
        cp_a(q).wait_recv()
        for k in (2, 1, 3):
            p = lax.rem(x + k, NX)
            sendb[q, k - 1] = add(wt[c, q, p], bufa[q, p])
            cp_b(q, k).start()
    def stage_c(q):
        for k in (1, 2, 3):
            cp_b(q, k).wait_recv()
        sendc[q] = add(wt[c, q, x], bufa[q, x], recvb[q, 0], recvb[q, 1], recvb[q, 2])
        cp_c(q).start()
    def stage_d(q):
        cp_c(q).wait_recv()
        wg[c, q, x] = add(sendc[q], recvc[q])
        for k in (2, 1, 3, 0):
            cp_d(q, k).start()
    def stage_e(q):
        for k in (1, 3, 2):
            arr_d(q, k).wait_recv()
            cp_e(q, k).start()

    def blk(i): return far_first(i, z)
    def cp_1(i, k):
        j = blk(i)
        src = pt.at[j * NY + y2, :, hi if k else lo]
        return remote(src, y1.at[i, k], s1.at[i, k], r1.at[i, k], ydev(ym if k else yp))
    def cp_2(i, k):
        return remote(sendy.at[i, k], recvy.at[i, k], s2.at[i, k], r2.at[i, k], ydev(ym if k else yp))
    def step_1(i):
        cp_1(i, 0).start(); cp_1(i, 1).start()
    def step_2(i):
        j = blk(i)
        cp_1(i, 0).wait_recv()
        sendy[i, 0, :, lo] = add(pt[j * NY + yp, :, lo], y1[i, 0])
        sendy[i, 0, :, hi] = pt[j * NY + yp, :, hi]
        cp_2(i, 0).start()
        cp_1(i, 1).wait_recv()
        sendy[i, 1, :, lo] = pt[j * NY + ym, :, lo]
        sendy[i, 1, :, hi] = add(pt[j * NY + ym, :, hi], y1[i, 1])
        cp_2(i, 1).start()
    def step_3(i):
        j = blk(i)
        cp_2(i, 0).wait_recv(); cp_2(i, 1).wait_recv()
        colsum[j] = add(pt[j * NY + y, :, :], recvy[i, 0], recvy[i, 1])
    def cp_z(j, t, dst):
        return remote(colsum.at[j], dst, szs.at[j], szr.at[j], zdev(t))
    def hop(j, sg, d):
        t = z + sg
        def plus():
            cp_z(j, t, zin.at[j]).wait_recv()
            colsum[j] = add(colsum[j], zin[j])
        when(has_r if sg < 0 else has_l, plus)
        if d == 1 and sg > 0:
            remote(colsum.at[j], zin2, szs.at[j], szr.at[NZ], zdev(t)).start()
        else:
            cp_z(j, t, zin.at[j]).start()
    def hops(d):
        for sg in (-1, 1):
            j = z + sg * d
            when(jnp.logical_and(j >= 0, j < NZ), functools.partial(hop, j, sg, d))
    def last():
        def from_right(): remote(zin.at[z], zin.at[z], szs.at[z], szr.at[z], zdev(z)).wait_recv()
        def from_left(): remote(zin2, zin2, szs.at[z], szr.at[NZ], zdev(z)).wait_recv()
        when(has_r, from_right)
        when(has_l, from_left)
        @pl.when(jnp.logical_and(has_l, has_r))
        def _(): pg[...] = add(colsum[z], zin[z], zin2[...])
        @pl.when(jnp.logical_not(has_l))
        def _(): pg[...] = add(colsum[z], zin[z])
        @pl.when(jnp.logical_not(has_r))
        def _(): pg[...] = add(colsum[z], zin2[...])

    for q in range(Q):
        cp_a(q).start()
    step_1(0); step_1(1)
    for e in range(NZ + 3):
        if e < Q: stage_b(e)
        if e == 0: step_2(0)
        if e + 2 < NZ: step_1(e + 2)
        if e + 1 < NZ: step_2(e + 1)
        if 1 <= e <= Q: stage_c(e - 1)
        if e < NZ:
            step_3(e)
            if e < NZ - 1: hops(NZ - 1 - e)
        if 4 <= e < 4 + Q: stage_d(e - 4)
        if 5 <= e < 5 + Q: stage_e(e - 5)
        if e == NZ - 1: last()
    for q in range(Q):
        arr_d(q, 0).wait_recv()
        for k in (1, 2, 3):
            arr_e(q, k).wait_recv()
    for q in range(Q):
        cp_a(q).wait_send(); cp_c(q).wait_send()
        for k in range(4): cp_d(q, k).wait_send()
        for k in (1, 2, 3):
            cp_b(q, k).wait_send(); cp_e(q, k).wait_send()
    for i in range(NZ):
        for k in (0, 1):
            cp_1(i, k).wait_send(); cp_2(i, k).wait_send()
        when(z != i, lambda i=i: cp_z(i, z, zin.at[i]).wait_send())

def reduce_all(pterm, wterm, Q=4, cid=1, name="reduce_grads"):
    nb, r, w = pterm.shape
    rows, cols = wterm.shape
    R = rows // (2 * Q * 4)
    D, S = pltpu.SemaphoreType.DMA, pltpu.VMEM
    pg, wg = pl.pallas_call(
        functools.partial(reduce_kernel, Q, R),
        out_shape=[jax.ShapeDtypeStruct((r, w), BF16), jax.ShapeDtypeStruct((2, Q, 4, R, cols), BF16)],
        in_specs=[pl.BlockSpec(memory_space=pltpu.VMEM)] * 2,
        out_specs=[pl.BlockSpec(memory_space=pltpu.VMEM)] * 2,
        scratch_shapes=[
            S((Q, 4, R, cols), BF16), S((Q, 3, R, cols), BF16), S((Q, 3, R, cols), BF16), S((Q, R, cols), BF16), S((Q, R, cols), BF16),
            S((NZ, 2, r, w // 2), BF16), S((NZ, 2, r, w), BF16), S((NZ, 2, r, w), BF16), S((NZ, r, w), BF16), S((NZ, r, w), BF16), S((r, w), BF16),
            D((Q,)), D((Q,)), D((Q, 3)), D((Q, 3)), D((Q,)), D((Q,)), D((Q, 4)), D((Q, 4)), D((Q, 3)), D((Q, 3)),
            D((NZ, 2)), D((NZ, 2)), D((NZ, 2)), D((NZ, 2)), D((NZ,)), D((NZ + 1,)),
        ],
        compiler_params=pltpu.CompilerParams(collective_id=cid, has_side_effects=True, vmem_limit_bytes=48 << 20),
        name=name,
    )(pterm, wterm.reshape(2, Q, 4, R, cols))
    return pg, wg.reshape(rows, cols)


def layer_normalize(values):
    centred = values - jnp.mean(values, axis=-1, keepdims=True)
    variance = jnp.mean(centred * centred, axis=-1, keepdims=True)
    rscale = lax.rsqrt(variance + 1e-06)
    return (centred * rscale, rscale)


def norm_backward(grads, normed, rscale):
    return (
        grads
        - jnp.mean(grads, axis=-1, keepdims=True)
        - normed * jnp.mean(grads * normed, axis=-1, keepdims=True)
    ) * rscale


def attention_back(qkv, context):
    rows_n = qkv.shape[0]
    heads = qkv.shape[1] // (3 * HD)
    split = qkv.reshape(rows_n, heads, 3, HD)
    query = split[:, :, 0, :].astype(jnp.float32)
    key_tensor = split[:, :, 1, :].astype(jnp.float32)
    values = split[:, :, 2, :]
    context = context.reshape(rows_n, heads, HD)
    qnorm, qscale = layer_normalize(query)
    normed_keys, key_scale = layer_normalize(key_tensor)
    rounded_queries = qnorm.astype(jnp.bfloat16)
    rounded_keys = normed_keys.astype(jnp.bfloat16)
    score_factor = 1.0 / HD**0.5
    logit_scores = (
        jnp.einsum(
            "wqg,zqg->qwz", rounded_queries, rounded_keys, preferred_element_type=jnp.float32
        )
        * score_factor
    )
    expo = jnp.exp(logit_scores)
    probs = expo / jnp.sum(expo, axis=-1, keepdims=True)
    pround = probs.astype(jnp.bfloat16)
    dsoft = jnp.einsum("wqg,zqg->qwz", context, values, preferred_element_type=jnp.float32)
    delta = jnp.sum(probs * dsoft, axis=-1, keepdims=True)
    score_grad = (probs * (dsoft - delta) * score_factor).astype(jnp.bfloat16)
    dvalue = jnp.einsum("hpj,phd->jhd", pround, context, preferred_element_type=jnp.float32)
    normed_query_grad = jnp.einsum(
        "rcw,wrt->crt", score_grad, rounded_keys, preferred_element_type=jnp.float32
    )
    normed_key_grad = jnp.einsum(
        "hpj,phd->jhd", score_grad, rounded_queries, preferred_element_type=jnp.float32
    )
    dquery = norm_backward(normed_query_grad, qnorm, qscale)
    key_cotangent = norm_backward(normed_key_grad, normed_keys, key_scale)
    joined = jnp.stack([dquery, key_cotangent, dvalue], axis=2)
    return joined.astype(jnp.bfloat16).reshape(rows_n, heads * 3 * HD)


def per_device(patches, qkv_weight, context_grad):
    gathered = gather_patches(patches, 2).reshape(-1, patches.shape[1])
    qkv = jnp.dot(gathered, qkv_weight, preferred_element_type=F32).astype(BF16)
    count = gathered.shape[0] // PATCHES
    qkv_images = qkv.reshape(count, PATCHES, qkv.shape[1])
    context_images = context_grad.reshape(count, PATCHES, context_grad.shape[1])
    qkv_grad = jax.vmap(attention_back)(qkv_images, context_images).reshape(
        gathered.shape[0], qkv.shape[1]
    )
    pterm = lax.dot_general(qkv_grad, qkv_weight, (((1,), (1,)), ((), ())), preferred_element_type=F32).astype(BF16)
    wterm = lax.dot_general(gathered, qkv_grad, (((0,), (0,)), ((), ())), preferred_element_type=F32).astype(BF16)
    return reduce_all(pterm.reshape(NZ * NY, -1, pterm.shape[1]), wterm)


def solution(mesh):
    in_specs = (P(("dp", "mp"), None), P(None, "mp"), P("dp", "mp"))
    out_specs = (P(("dp", "mp"), None), P(None, "mp"))
    return jax.shard_map(
        per_device, mesh=mesh, in_specs=in_specs, out_specs=out_specs, check_vma=False
    )
```

```python
import functools
import jax
import jax.numpy as jnp
from jax import lax
from jax.experimental import pallas as pl
from jax.experimental.pallas import tpu as pltpu
from jax.sharding import PartitionSpec as P

MESH = pl.DeviceIdType.MESH
NZ, NY, NX = 8, 4, 4
HD = 128
PATCHES = 256
STRIDE = 2
Q = 4
F32, BF16 = jnp.float32, jnp.bfloat16


def when(cond, fn):
    pl.when(cond)(fn)


def add(*terms):
    total = terms[0].astype(F32)
    for t in terms[1:]:
        total = total + t.astype(F32)
    return total.astype(BF16)


def dot(a, b, dims):
    return lax.dot_general(a, b, (dims, ((), ())), preferred_element_type=F32)


def normalize(t):
    t = t.astype(F32)
    centred = t - jnp.mean(t, axis=-1, keepdims=True)
    r = lax.rsqrt(jnp.mean(centred * centred, axis=-1, keepdims=True) + 1e-06)
    return centred * r, r


def norm_back(g, n, r):
    return (g - jnp.mean(g, axis=-1, keepdims=True) - n * jnp.mean(g * n, axis=-1, keepdims=True)) * r


def attend(qkv, ctx):
    qn, qr = normalize(qkv[:, :HD])
    kn, kr = normalize(qkv[:, HD : 2 * HD])
    v = qkv[:, 2 * HD :]
    qb, kb = qn.astype(BF16), kn.astype(BF16)
    f = 1.0 / HD**0.5
    ex = jnp.exp(dot(kb, qb, ((1,), (1,))) * f)
    p = ex / jnp.sum(ex, axis=0, keepdims=True)
    dsoft = dot(v, ctx, ((1,), (1,)))
    delta = jnp.sum(p * dsoft, axis=0, keepdims=True)
    ds = (p * (dsoft - delta) * f).astype(BF16)
    dv = dot(p.astype(BF16), ctx, ((1,), (0,)))
    dkn = dot(ds, qb, ((1,), (0,)))
    dqn = dot(ds, kb, ((0,), (0,)))
    return jnp.concatenate(
        [norm_back(dqn, qn, qr).astype(BF16), norm_back(dkn, kn, kr).astype(BF16), dv.astype(BF16)], axis=1
    )


def far_first(i, z):
    right = z >= NZ // 2
    near = jnp.where(right, z, NZ - 1 - z)
    alone = 2 * near - (NZ - 1)
    over = jnp.maximum(i - alone, 0)
    d = (NZ - 1 - near) - over // 2
    j = jnp.where(i < alone, i, jnp.where(over % 2 == 0, near - d, near + d))
    return jnp.where(right, j, NZ - 1 - j)


def kernel(x_ref, w_ref, ctx_ref, pg, wg,
           g, qg, w_t, pt, wts, wto,
           bufa, sendb, recvb, sendc, recvc, y1, sendy, recvy, colsum, zin, zin2,
           lsem, gzs, gzr, gys, gyr,
           sa, ra, sb, rb, sc, rc, sd, rd, se, re, s1, r1, s2, r2, szs, szr):
    dp = lax.axis_index("dp")
    mp = lax.axis_index("mp")
    x, zh, c = dp // 4, lax.rem(dp // 2, 2), lax.rem(dp, 2)
    z, y = mp // NY, lax.rem(mp, NY)
    yp, ym, y2 = lax.rem(y + 1, NY), lax.rem(y + NY - 1, NY), lax.rem(y + 2, NY)
    depth = x_ref.shape[1]
    rows = x_ref.shape[0]
    half = depth // 2
    part = depth // (2 * Q)
    lo, hi = pl.ds(0, half), pl.ds(half, half)
    sib = (x * 4 + zh * 2 + (1 - c), mp)
    far = (x * 4 + (1 - zh) * 2 + c, mp)

    def xdev(k): return (lax.rem(x + k, NX) * 4 + zh * 2 + c, mp)
    def ydev(t): return (dp, z * NY + t)
    def zdev(t): return (dp, t * NY + y)
    def ok(t): return jnp.logical_and(t >= 0, t < NZ)
    def remote(src, dst, ss, rs, dev):
        return pltpu.make_async_remote_copy(src, dst, ss, rs, device_id=dev, device_id_type=MESH)

    own = pltpu.make_async_copy(x_ref, g.at[mp], lsem)
    own.start()
    bar = pltpu.get_barrier_semaphore()
    for dev in (sib, far, xdev(1), xdev(2), xdev(3), ydev(yp), ydev(ym)):
        pl.semaphore_signal(bar, inc=1, device_id=dev, device_id_type=MESH)
    count = jnp.int32(7)
    for s in range(1, STRIDE + 1):
        for t in (z - s, z + s):
            when(ok(t), lambda t=t: pl.semaphore_signal(bar, inc=1, device_id=zdev(t), device_id_type=MESH))
            count = count + ok(t).astype(jnp.int32)
    pl.semaphore_wait(bar, count)
    own.wait()

    def zcopy(j, t, k):
        b = g.at[j * NY + y]
        return remote(b, b, gzs.at[j, k], gzr.at[j], zdev(t))
    def ypiece(j, k):
        b = g.at[j * NY + (ym, yp, y2, y2)[k]]
        return b if k < 2 else b.at[:, (lo, hi)[k - 2]]
    def ycopy(j, k):
        if k < 2:
            b = g.at[j * NY + y]
        else:
            b = g.at[j * NY + (ym, yp)[k - 2], :, (lo, hi)[k - 2]]
        return remote(b, b, gys.at[j, k], gyr.at[j, k], ydev((yp, ym)[k % 2]))
    def yarrive(j, k):
        b = ypiece(j, k)
        return remote(b, b, gys.at[j, k], gyr.at[j, k], ydev(yp))
    def forward(j):
        yarrive(j, 0).wait_recv()
        ycopy(j, 2).start()
        yarrive(j, 1).wait_recv()
        ycopy(j, 3).start()

    for s in range(1, STRIDE + 1):
        for i, sg in enumerate((-1, 1)):
            t = z + sg * s
            when(ok(t), lambda t=t, k=2 * (s - 1) + i: zcopy(z, t, k).start())
    ycopy(z, 0).start()
    ycopy(z, 1).start()
    w_t[...] = w_ref[...].T
    for d in range(1, NZ):
        for sg in (-1, 1):
            j = z + sg * d
            def take(j=j, sg=sg, d=d):
                zcopy(j, z, 0).wait_recv()
                if d % STRIDE == 0:
                    for s in range(1, STRIDE + 1):
                        t = z - sg * s
                        when(ok(t), lambda t=t, s=s: zcopy(j, t, s - 1).start())
                ycopy(j, 0).start()
                ycopy(j, 1).start()
            when(ok(j), take)
        if d == 1:
            forward(z)
        else:
            for sg in (-1, 1):
                j = z + sg * (d - 1)
                when(ok(j), functools.partial(forward, j))
    for sg in (-1, 1):
        j = z + sg * (NZ - 1)
        when(ok(j), functools.partial(forward, j))

    near = z // (NZ // 2)
    blocks = PATCHES // rows
    for image in (near, 1 - near):
        for i in range(NZ // 2):
            j = image * (NZ // 2) + i
            yarrive(j, 2).wait_recv()
            yarrive(j, 3).wait_recv()
        first = pl.multiple_of(image * PATCHES, PATCHES)
        qkv = dot(g[pl.ds(image * blocks, blocks)].reshape(PATCHES, depth), w_ref[...], ((1,), (0,))).astype(BF16)
        qg[pl.ds(first, PATCHES), :] = attend(qkv, ctx_ref[pl.ds(first, PATCHES), :])

    tokens = g.shape[0] * rows
    def weight_term(h, q):
        cols = pl.ds(pl.multiple_of(h * half + q * part, part), part)
        return dot(g[:, :, cols].reshape(tokens, part), qg[...], ((0,), (0,))).astype(BF16).reshape(wts.shape[1:])
    def cp_a(q): return remote(wts.at[q], bufa.at[q], sa.at[q], ra.at[q], sib)
    def cp_b(q, k): return remote(sendb.at[q, k - 1], recvb.at[q, k - 1], sb.at[q, k - 1], rb.at[q, k - 1], xdev(k))
    def cp_c(q): return remote(sendc.at[q], recvc.at[q], sc.at[q], rc.at[q], far)
    def cp_d(q, k):
        b = wg.at[c, q, x]
        return remote(b, b, sd.at[q, k], rd.at[q, k], sib if k == 0 else xdev(k))
    def arr_d(q, k):
        b = wg.at[1 - c, q, x] if k == 0 else wg.at[c, q, lax.rem(x + NX - k, NX)]
        return remote(b, b, sd.at[q, k], rd.at[q, k], sib)
    def cp_e(q, k):
        b = wg.at[c, q, lax.rem(x + NX - k, NX)]
        return remote(b, b, se.at[q, k - 1], re.at[q, k - 1], sib)
    def arr_e(q, k):
        b = wg.at[1 - c, q, lax.rem(x + NX - k, NX)]
        return remote(b, b, se.at[q, k - 1], re.at[q, k - 1], sib)
    def stage_a(q):
        wts[q] = weight_term(1 - c, q)
        cp_a(q).start()
    def stage_b(q):
        wto[q] = weight_term(c, q)
        cp_a(q).wait_recv()
        for k in (2, 1, 3):
            p = lax.rem(x + k, NX)
            sendb[q, k - 1] = add(wto[q, p], bufa[q, p])
            cp_b(q, k).start()
    def stage_c(q):
        for k in (1, 2, 3):
            cp_b(q, k).wait_recv()
        sendc[q] = add(wto[q, x], bufa[q, x], recvb[q, 0], recvb[q, 1], recvb[q, 2])
        cp_c(q).start()
    def stage_d(q):
        cp_c(q).wait_recv()
        wg[c, q, x] = add(sendc[q], recvc[q])
        for k in (2, 1, 3, 0):
            cp_d(q, k).start()
    def stage_e(q):
        for k in (1, 3, 2):
            arr_d(q, k).wait_recv()
            cp_e(q, k).start()

    def blk(i): return far_first(i, z)
    def cp_1(i, k):
        src = pt.at[i, y2, :, hi if k else lo]
        return remote(src, y1.at[i, k], s1.at[i, k], r1.at[i, k], ydev(ym if k else yp))
    def cp_2(i, k):
        return remote(sendy.at[i, k], recvy.at[i, k], s2.at[i, k], r2.at[i, k], ydev(ym if k else yp))
    def step_1(i):
        some = NY * rows
        first = pl.multiple_of(blk(i) * some, some)
        pt[i] = dot(qg[pl.ds(first, some), :], w_t[...], ((1,), (0,))).astype(BF16).reshape(NY, rows, depth)
        cp_1(i, 0).start()
        cp_1(i, 1).start()
    def step_2(i):
        cp_1(i, 0).wait_recv()
        sendy[i, 0, :, lo] = add(pt[i, yp, :, lo], y1[i, 0])
        sendy[i, 0, :, hi] = pt[i, yp, :, hi]
        cp_2(i, 0).start()
        cp_1(i, 1).wait_recv()
        sendy[i, 1, :, lo] = pt[i, ym, :, lo]
        sendy[i, 1, :, hi] = add(pt[i, ym, :, hi], y1[i, 1])
        cp_2(i, 1).start()
    def step_3(i):
        cp_2(i, 0).wait_recv()
        cp_2(i, 1).wait_recv()
        colsum[blk(i)] = add(pt[i, y], recvy[i, 0], recvy[i, 1])
    def cp_z(j, t, dst):
        return remote(colsum.at[j], dst, szs.at[j], szr.at[j], zdev(t))
    has_l, has_r = z > 0, z < NZ - 1
    def hop(j, sg, d):
        t = z + sg
        def plus():
            cp_z(j, t, zin.at[j]).wait_recv()
            colsum[j] = add(colsum[j], zin[j])
        when(has_r if sg < 0 else has_l, plus)
        if d == 1 and sg > 0:
            remote(colsum.at[j], zin2, szs.at[j], szr.at[NZ], zdev(t)).start()
        else:
            cp_z(j, t, zin.at[j]).start()
    def hops(d):
        for sg in (-1, 1):
            j = z + sg * d
            when(ok(j), functools.partial(hop, j, sg, d))
    def last():
        when(has_r, lambda: remote(zin.at[z], zin.at[z], szs.at[z], szr.at[z], zdev(z)).wait_recv())
        when(has_l, lambda: remote(zin2, zin2, szs.at[z], szr.at[NZ], zdev(z)).wait_recv())
        @pl.when(jnp.logical_and(has_l, has_r))
        def _(): pg[...] = add(colsum[z], zin[z], zin2[...])
        @pl.when(jnp.logical_not(has_l))
        def _(): pg[...] = add(colsum[z], zin[z])
        @pl.when(jnp.logical_not(has_r))
        def _(): pg[...] = add(colsum[z], zin2[...])

    stage_a(0)
    step_1(0)
    stage_a(1)
    step_1(1)
    for q in range(2, Q):
        stage_a(q)
    for e in range(NZ + 3):
        if e < Q: stage_b(e)
        if e == 0: step_2(0)
        if e + 2 < NZ: step_1(e + 2)
        if e + 1 < NZ: step_2(e + 1)
        if 1 <= e <= Q: stage_c(e - 1)
        if e < NZ:
            step_3(e)
            if e < NZ - 1: hops(NZ - 1 - e)
        if 4 <= e < 4 + Q: stage_d(e - 4)
        if 5 <= e < 5 + Q: stage_e(e - 5)
        if e == NZ - 1: last()

    for q in range(Q):
        arr_d(q, 0).wait_recv()
        for k in (1, 2, 3):
            arr_e(q, k).wait_recv()
    for q in range(Q):
        cp_a(q).wait_send()
        cp_c(q).wait_send()
        for k in range(4):
            cp_d(q, k).wait_send()
        for k in (1, 2, 3):
            cp_b(q, k).wait_send()
            cp_e(q, k).wait_send()
    for i in range(NZ):
        for k in (0, 1):
            cp_1(i, k).wait_send()
            cp_2(i, k).wait_send()
        for k in range(4):
            ycopy(i, k).wait_send()
        when(z != i, lambda i=i: cp_z(i, z, zin.at[i]).wait_send())
    for s in range(1, STRIDE + 1):
        for i, sg in enumerate((-1, 1)):
            t = z + sg * s
            when(ok(t), lambda t=t, k=2 * (s - 1) + i: zcopy(z, t, k).wait_send())
    for d in range(STRIDE, NZ, STRIDE):
        for sg in (-1, 1):
            j = z + sg * d
            for s in range(1, STRIDE + 1):
                t = z - sg * s
                when(jnp.logical_and(ok(j), ok(t)), lambda j=j, t=t, s=s: zcopy(j, t, s - 1).wait_send())


def per_device(patches, qkv_weight, context_grad):
    rows, depth = patches.shape
    cols = qkv_weight.shape[1]
    R = depth // (2 * Q * NX)
    D, S = pltpu.SemaphoreType.DMA, pltpu.VMEM
    def buf(*shape): return S(shape, BF16)
    pg, wg = pl.pallas_call(
        kernel,
        out_shape=[jax.ShapeDtypeStruct((rows, depth), BF16), jax.ShapeDtypeStruct((2, Q, NX, R, cols), BF16)],
        in_specs=[pl.BlockSpec(memory_space=pltpu.VMEM)] * 3,
        out_specs=[pl.BlockSpec(memory_space=pltpu.VMEM)] * 2,
        scratch_shapes=[
            buf(NZ * NY, rows, depth), buf(NZ * NY * rows, cols), buf(cols, depth), buf(NZ, NY, rows, depth),
            buf(Q, NX, R, cols), buf(Q, NX, R, cols),
            buf(Q, NX, R, cols), buf(Q, 3, R, cols), buf(Q, 3, R, cols), buf(Q, R, cols), buf(Q, R, cols),
            buf(NZ, 2, rows, depth // 2), buf(NZ, 2, rows, depth), buf(NZ, 2, rows, depth),
            buf(NZ, rows, depth), buf(NZ, rows, depth), buf(rows, depth),
            D, D((NZ, 2 * STRIDE)), D((NZ,)), D((NZ, 4)), D((NZ, 4)),
            D((Q,)), D((Q,)), D((Q, 3)), D((Q, 3)), D((Q,)), D((Q,)), D((Q, 4)), D((Q, 4)), D((Q, 3)), D((Q, 3)),
            D((NZ, 2)), D((NZ, 2)), D((NZ, 2)), D((NZ, 2)), D((NZ,)), D((NZ + 1,)),
        ],
        compiler_params=pltpu.CompilerParams(collective_id=1, has_side_effects=True, vmem_limit_bytes=56 << 20),
        name="attention_back",
    )(patches, qkv_weight, context_grad)
    return pg, wg.reshape(depth, cols)


def solution(mesh):
    in_specs = (P(("dp", "mp"), None), P(None, "mp"), P("dp", "mp"))
    out_specs = (P(("dp", "mp"), None), P(None, "mp"))
    return jax.shard_map(
        per_device, mesh=mesh, in_specs=in_specs, out_specs=out_specs, check_vma=False
    )
```

```python
import functools
import jax
import jax.numpy as jnp
from jax import lax
from jax.experimental import pallas as pl
from jax.experimental.pallas import tpu as pltpu
from jax.sharding import PartitionSpec as P

MESH = pl.DeviceIdType.MESH
NZ, NY, NX = 8, 4, 4
HD = 128
PATCHES = 256
Q = 6
DIRECT = 6
T_A, T_B, T_C, T_D, T_E = 0.0, 3.5, 8.5, 28.0, 33.0
B_STEP, D_STEP = 12.4, 28.0
Y1, Y2, Y3, Y_STEP = 1.0, 5.5, 11.0, 3.1
Z_AT = (0, 0, 0, 0, 24, 27, 33, 60)
F32, BF16 = jnp.float32, jnp.bfloat16


def add(*terms):
    total = terms[0].astype(F32)
    for t in terms[1:]:
        total = total + t.astype(F32)
    return total.astype(BF16)


def dot(a, b, dims):
    return lax.dot_general(a, b, (dims, ((), ())), preferred_element_type=F32)


def normalize(t):
    t = t.astype(F32)
    centred = t - jnp.mean(t, axis=-1, keepdims=True)
    r = lax.rsqrt(jnp.mean(centred * centred, axis=-1, keepdims=True) + 1e-06)
    return centred * r, r


def norm_back(g, n, r):
    return (g - jnp.mean(g, axis=-1, keepdims=True) - n * jnp.mean(g * n, axis=-1, keepdims=True)) * r


def attend(qkv, ctx):
    qn, qr = normalize(qkv[:, :HD])
    kn, kr = normalize(qkv[:, HD : 2 * HD])
    v = qkv[:, 2 * HD :]
    qb, kb = qn.astype(BF16), kn.astype(BF16)
    f = 1.0 / HD**0.5
    ex = jnp.exp(dot(kb, qb, ((1,), (1,))) * f)
    p = ex / jnp.sum(ex, axis=0, keepdims=True)
    dsoft = dot(v, ctx, ((1,), (1,)))
    delta = jnp.sum(p * dsoft, axis=0, keepdims=True)
    ds = (p * (dsoft - delta) * f).astype(BF16)
    dv = dot(p.astype(BF16), ctx, ((1,), (0,)))
    dkn = dot(ds, qb, ((1,), (0,)))
    dqn = dot(ds, kb, ((0,), (0,)))
    return jnp.concatenate(
        [norm_back(dqn, qn, qr).astype(BF16), norm_back(dkn, kn, kr).astype(BF16), dv.astype(BF16)], axis=1
    )


def flip(z, m):
    return sum(lax.rem(z // k + m // k % 2, 2) * k for k in (1, 2, 4))


def kernel(x_ref, w_hbm, ctx_hbm, pg, wg,
           w_ref, ctx_ref, g, qg, w_t, pt, wts, wto,
           bufa, sendb, recvb, sendc, recvc, y1, sendy, recvy, sendz, recvz,
           lsem, far_sem, gzs, gzr, gys, gyr,
           sa, ra, sb, rb, sc, rc, sd, rd, se, re, s1, r1, s2, r2, szs, szr):
    dp = lax.axis_index("dp")
    mp = lax.axis_index("mp")
    x, zh, c = dp // 4, lax.rem(dp // 2, 2), lax.rem(dp, 2)
    z, y = mp // NY, lax.rem(mp, NY)
    yp, ym, y2 = lax.rem(y + 1, NY), lax.rem(y + NY - 1, NY), lax.rem(y + 2, NY)
    depth = x_ref.shape[1]
    rows = x_ref.shape[0]
    half = depth // 2
    part = depth // (2 * Q)
    lo, hi = pl.ds(0, half), pl.ds(half, half)
    sib = (x * 4 + zh * 2 + (1 - c), mp)
    far = (x * 4 + (1 - zh) * 2 + c, mp)

    def xdev(k): return (lax.rem(x + k, NX) * 4 + zh * 2 + c, mp)
    def ydev(t): return (dp, z * NY + t)
    def zdev(m): return (dp, flip(z, m) * NY + y)
    def remote(src, dst, ss, rs, dev):
        return pltpu.make_async_remote_copy(src, dst, ss, rs, device_id=dev, device_id_type=MESH)

    own = pltpu.make_async_copy(x_ref, g.at[mp], lsem.at[0])
    load_w = pltpu.make_async_copy(w_hbm, w_ref, lsem.at[1])
    load_ctx = pltpu.make_async_copy(ctx_hbm, ctx_ref, lsem.at[2])
    own.start()
    load_w.start()
    load_ctx.start()
    def ring(k):
        t = lax.rem(zh * NZ + z + k + 2 * NZ, 2 * NZ)
        return (x * 4 + t // NZ * 2 + c, lax.rem(t, NZ) * NY + y)
    bar = pltpu.get_barrier_semaphore()
    relays = (ring(4), ring(-4))
    partners = (ydev(yp), ydev(ym), ydev(y2), ring(1), ring(-1), ring(2), ring(-2), sib, xdev(1), xdev(2), xdev(3), *relays)
    for dev in partners:
        pl.semaphore_signal(bar, inc=1, device_id=dev, device_id_type=MESH)
    pl.semaphore_wait(bar, len(partners))
    for dev in relays:
        pl.semaphore_signal(far_sem, inc=1, device_id=dev, device_id_type=MESH)
    own.wait()

    def ok(t): return jnp.logical_and(t >= 0, t < NZ)
    def when(cond, f, *args): pl.when(cond)(functools.partial(f, *args))
    def direct(d): return d >= DIRECT
    def zcopy(j, t, k):
        b = g.at[j * NY + y]
        return remote(b, b, gzs.at[j, k], gzr.at[j], (dp, t * NY + y))
    def ycopy(j, k):
        b = g.at[j * NY + (ym, yp)[k - 2], :, (lo, hi)[k - 2]] if k in (2, 3) else g.at[j * NY + y]
        return remote(b, b, gys.at[j, k], gyr.at[j, k], ydev((yp, ym, yp, ym, y2)[k]))
    def yarrive(j, k):
        b = g.at[j * NY + (ym, yp, y2, y2, y2)[k]]
        b = b.at[:, (lo, hi)[k - 2]] if k in (2, 3) else b
        return remote(b, b, gys.at[j, k], gyr.at[j, k], ydev(yp))
    def spread(j, d):
        for k in (4, 0, 1) if direct(d) else (0, 1):
            ycopy(j, k).start()
    def forward(j):
        yarrive(j, 0).wait_recv()
        ycopy(j, 2).start()
        yarrive(j, 1).wait_recv()
        ycopy(j, 3).start()
    def take(j, sg, d):
        zcopy(j, z, 0).wait_recv()
        if d % 2 == 0:
            for s in (1, 2):
                t = z - sg * s
                when(ok(t), lambda t, s: zcopy(j, t, s - 1).start(), t, s)
        spread(j, d)
    def complete(j, d):
        for k in (0, 1, 4) if direct(d) else (2, 3):
            yarrive(j, k).wait_recv()

    blocks = PATCHES // rows
    near = z // (NZ // 2)
    def image_back(image):
        first = pl.multiple_of(image * PATCHES, PATCHES)
        qkv = dot(g[pl.ds(image * blocks, blocks)].reshape(PATCHES, depth), w_ref[...], ((1,), (0,))).astype(BF16)
        qg[pl.ds(first, PATCHES), :] = attend(qkv, ctx_ref[pl.ds(first, PATCHES), :])

    sides = (-1, 1)
    for s in (1, 2):
        for i, sg in enumerate(sides):
            t = z + sg * s
            when(ok(t), lambda t, k: zcopy(z, t, k).start(), t, 2 * (s - 1) + i)
    spread(z, 0)
    load_w.wait()
    load_ctx.wait()
    w_t[...] = w_ref[...].T
    for d in range(1, NZ):
        for sg in sides:
            j = z + sg * d
            when(ok(j), take, j, sg, d)
        if not direct(d - 1):
            if d == 1:
                forward(z)
            else:
                for sg in sides:
                    j = z + sg * (d - 1)
                    when(ok(j), forward, j)
    if not direct(NZ - 1):
        for sg in sides:
            j = z + sg * (NZ - 1)
            when(ok(j), forward, j)
    def complete_all(ds, inside):
        for d in ds:
            for sg in sides if d else (1,):
                j = z + sg * d
                same = (j // (NZ // 2) == near) if inside else (j // (NZ // 2) != near)
                when(jnp.logical_and(ok(j), same), complete, j, d)
    complete_all(range(NZ // 2), True)
    image_back(near)
    complete_all(range(1, NZ), False)
    image_back(1 - near)

    tokens = g.shape[0] * rows
    def weight_term(h, q):
        cols = pl.ds(pl.multiple_of(h * half + q * part, part), part)
        return dot(g[:, :, cols].reshape(tokens, part), qg[...], ((0,), (0,))).astype(BF16).reshape(wts.shape[1:])
    def cp_a(q): return remote(wts.at[q], bufa.at[q], sa.at[q], ra.at[q], sib)
    def cp_b(q, k): return remote(sendb.at[q, k - 1], recvb.at[q, k - 1], sb.at[q, k - 1], rb.at[q, k - 1], xdev(k))
    def cp_c(q): return remote(sendc.at[q], recvc.at[q], sc.at[q], rc.at[q], far)
    def cp_d(q, k):
        b = wg.at[c, q, x]
        return remote(b, b, sd.at[q, k], rd.at[q, k], sib if k == 0 else xdev(k))
    def arr_d(q, k):
        b = wg.at[1 - c, q, x] if k == 0 else wg.at[c, q, lax.rem(x + NX - k, NX)]
        return remote(b, b, sd.at[q, k], rd.at[q, k], sib)
    def cp_e(q, k):
        b = wg.at[c, q, lax.rem(x + NX - k, NX)]
        return remote(b, b, se.at[q, k - 1], re.at[q, k - 1], sib)
    def arr_e(q, k):
        b = wg.at[1 - c, q, lax.rem(x + NX - k, NX)]
        return remote(b, b, se.at[q, k - 1], re.at[q, k - 1], sib)
    def stage_a(q):
        wts[q] = weight_term(1 - c, q)
        cp_a(q).start()
    def stage_b(q):
        wto[q] = weight_term(c, q)
        cp_a(q).wait_recv()
        for k in (2, 1, 3):
            p = lax.rem(x + k, NX)
            sendb[q, k - 1] = add(wto[q, p], bufa[q, p])
            cp_b(q, k).start()
    def stage_c(q):
        if q == 0:
            pl.semaphore_wait(far_sem, len(relays))
        for k in (1, 2, 3):
            cp_b(q, k).wait_recv()
        sendc[q] = add(wto[q, x], bufa[q, x], recvb[q, 0], recvb[q, 1], recvb[q, 2])
        cp_c(q).start()
    def stage_d(q):
        cp_c(q).wait_recv()
        wg[c, q, x] = add(sendc[q], recvc[q])
        for k in (2, 1, 3, 0):
            cp_d(q, k).start()
    def stage_e(q):
        for k in (1, 3, 2):
            arr_d(q, k).wait_recv()
            cp_e(q, k).start()

    order = (7, 3, 5, 1, 6, 2, 4, 0)
    def cp_1(i, k):
        src = pt.at[i, y2, :, hi if k else lo]
        return remote(src, y1.at[i, k], s1.at[i, k], r1.at[i, k], ydev(ym if k else yp))
    def cp_2(i, k):
        return remote(sendy.at[i, k], recvy.at[i, k], s2.at[i, k], r2.at[i, k], ydev(ym if k else yp))
    def step_1(i):
        some = NY * rows
        first = pl.multiple_of(flip(z, order[i]) * some, some)
        pt[i] = dot(qg[pl.ds(first, some), :], w_t[...], ((1,), (0,))).astype(BF16).reshape(NY, rows, depth)
        cp_1(i, 0).start()
        cp_1(i, 1).start()
    def step_2(i):
        cp_1(i, 0).wait_recv()
        sendy[i, 0, :, lo] = add(pt[i, yp, :, lo], y1[i, 0])
        sendy[i, 0, :, hi] = pt[i, yp, :, hi]
        cp_2(i, 0).start()
        cp_1(i, 1).wait_recv()
        sendy[i, 1, :, lo] = pt[i, ym, :, lo]
        sendy[i, 1, :, hi] = add(pt[i, ym, :, hi], y1[i, 1])
        cp_2(i, 1).start()
    def cp_z(i):
        to, slot = ((1, i), (2, i), (4, 6))[(i >= 4) + (i >= 6)]
        return remote(sendz.at[i], recvz.at[slot], szs.at[slot], szr.at[slot], zdev(to))
    extra = {4: (0,), 5: (1,), 6: (2, 4), 7: (3, 5, 6)}
    def step_3(i):
        cp_2(i, 0).wait_recv()
        cp_2(i, 1).wait_recv()
        for slot in extra.get(i, ()):
            cp_z(slot).wait_recv()
        total = add(pt[i, y], recvy[i, 0], recvy[i, 1], *[recvz[slot] for slot in extra.get(i, ())])
        if i == NZ - 1:
            pg[...] = total
        else:
            sendz[i] = total
            cp_z(i).start()

    steps = []
    def at(t, f, i): steps.append((t, len(steps), f, i))
    for q in range(Q):
        at(T_A + 1.7 / Q * q, stage_a, q)
        at(T_B + B_STEP / Q * q, stage_b, q)
        at(T_C + B_STEP / Q * q, stage_c, q)
        at(T_D + D_STEP / Q * q, stage_d, q)
        at(T_E + D_STEP / Q * q, stage_e, q)
    for i in range(NZ):
        at(Y1 + Y_STEP * i, step_1, i)
        at(Y2 + Y_STEP * i, step_2, i)
        at(max(Y3 + Y_STEP * i, Z_AT[i]), step_3, i)
    for t, n, f, i in sorted(steps, key=lambda s: s[:2]):
        f(i)

    for q in range(Q):
        arr_d(q, 0).wait_recv()
        for k in (1, 2, 3):
            arr_e(q, k).wait_recv()
    for q in range(Q):
        cp_a(q).wait_send()
        cp_c(q).wait_send()
        for k in range(4):
            cp_d(q, k).wait_send()
        for k in (1, 2, 3):
            cp_b(q, k).wait_send()
            cp_e(q, k).wait_send()
    for i in range(NZ):
        for k in (0, 1):
            cp_1(i, k).wait_send()
            cp_2(i, k).wait_send()
        if i < NZ - 1:
            cp_z(i).wait_send()
    for d in range(NZ):
        for sg in sides if d else (1,):
            j = z + sg * d
            def sent(j, sg, d):
                for k in (0, 1, 4) if direct(d) else range(4):
                    ycopy(j, k).wait_send()
                if d and d % 2 == 0:
                    for s in (1, 2):
                        when(ok(z - sg * s), lambda s: zcopy(j, z, s - 1).wait_send(), s)
            when(ok(j), sent, j, sg, d)
    for s in (1, 2):
        for i, sg in enumerate(sides):
            when(ok(z + sg * s), lambda k: zcopy(z, z, k).wait_send(), 2 * (s - 1) + i)


def per_device(patches, qkv_weight, context_grad):
    rows, depth = patches.shape
    cols = qkv_weight.shape[1]
    R = depth // (2 * Q * NX)
    D, S = pltpu.SemaphoreType.DMA, pltpu.VMEM
    def buf(*shape): return S(shape, BF16)
    pg, wg = pl.pallas_call(
        kernel,
        out_shape=[jax.ShapeDtypeStruct((rows, depth), BF16), jax.ShapeDtypeStruct((2, Q, NX, R, cols), BF16)],
        in_specs=[pl.BlockSpec(memory_space=pltpu.HBM)] * 3,
        out_specs=[pl.BlockSpec(memory_space=pltpu.VMEM)] * 2,
        scratch_shapes=[
            buf(depth, cols), buf(*context_grad.shape), buf(NZ * NY, rows, depth), buf(NZ * NY * rows, cols), buf(cols, depth), buf(NZ, NY, rows, depth),
            buf(Q, NX, R, cols), buf(Q, NX, R, cols),
            buf(Q, NX, R, cols), buf(Q, 3, R, cols), buf(Q, 3, R, cols), buf(Q, R, cols), buf(Q, R, cols),
            buf(NZ, 2, rows, depth // 2), buf(NZ, 2, rows, depth), buf(NZ, 2, rows, depth),
            buf(NZ - 1, rows, depth), buf(NZ - 1, rows, depth),
            D((3,)), pltpu.SemaphoreType.REGULAR, D((NZ, 4)), D((NZ,)), D((NZ, 5)), D((NZ, 5)),
            D((Q,)), D((Q,)), D((Q, 3)), D((Q, 3)), D((Q,)), D((Q,)), D((Q, 4)), D((Q, 4)), D((Q, 3)), D((Q, 3)),
            D((NZ, 2)), D((NZ, 2)), D((NZ, 2)), D((NZ, 2)), D((NZ - 1,)), D((NZ - 1,)),
        ],
        compiler_params=pltpu.CompilerParams(collective_id=1, has_side_effects=True, vmem_limit_bytes=30 << 20),
        name="attention_back",
    )(patches, qkv_weight, context_grad)
    return pg, wg.reshape(depth, cols)


def solution(mesh):
    in_specs = (P(("dp", "mp"), None), P(None, "mp"), P("dp", "mp"))
    out_specs = (P(("dp", "mp"), None), P(None, "mp"))
    return jax.shard_map(
        per_device, mesh=mesh, in_specs=in_specs, out_specs=out_specs, check_vma=False
    )
```

```python
import functools
import jax
import jax.numpy as jnp
from jax import lax
from jax.experimental import pallas as pl
from jax.experimental.pallas import tpu as pltpu
from jax.sharding import PartitionSpec as P

MESH = pl.DeviceIdType.MESH
NZ, NY, NX = 8, 4, 4
HD = 128
PATCHES = 256
Q, GROUP = 6, 1
DIRECT = 6
T_A, T_B, T_C, T_D, T_E = 0.0, 3.5, 8.5, 28.0, 33.0
B_STEP, D_STEP = 12.4, 28.0
Y1, Y2, Y3, Y_STEP = 1.0, 5.5, 11.0, 3.1
Z_AT = (0, 0, 0, 0, 24, 27, 33, 60)
F32, BF16 = jnp.float32, jnp.bfloat16


def add(*terms):
    total = terms[0].astype(F32)
    for t in terms[1:]:
        total = total + t.astype(F32)
    return total.astype(BF16)


def dot(a, b, dims):
    return lax.dot_general(a, b, (dims, ((), ())), preferred_element_type=F32)


def normalize(t):
    t = t.astype(F32)
    centred = t - jnp.mean(t, axis=-1, keepdims=True)
    r = lax.rsqrt(jnp.mean(centred * centred, axis=-1, keepdims=True) + 1e-06)
    return centred * r, r


def norm_back(g, n, r):
    return (g - jnp.mean(g, axis=-1, keepdims=True) - n * jnp.mean(g * n, axis=-1, keepdims=True)) * r


def attend(qkv, ctx):
    qn, qr = normalize(qkv[:, :HD])
    kn, kr = normalize(qkv[:, HD : 2 * HD])
    v = qkv[:, 2 * HD :]
    qb, kb = qn.astype(BF16), kn.astype(BF16)
    f = 1.0 / HD**0.5
    ex = jnp.exp(dot(kb, qb, ((1,), (1,))) * f)
    p = ex / jnp.sum(ex, axis=0, keepdims=True)
    dsoft = dot(v, ctx, ((1,), (1,)))
    delta = jnp.sum(p * dsoft, axis=0, keepdims=True)
    ds = (p * (dsoft - delta) * f).astype(BF16)
    dv = dot(p.astype(BF16), ctx, ((1,), (0,)))
    dkn = dot(ds, qb, ((1,), (0,)))
    dqn = dot(ds, kb, ((0,), (0,)))
    return jnp.concatenate(
        [norm_back(dqn, qn, qr).astype(BF16), norm_back(dkn, kn, kr).astype(BF16), dv.astype(BF16)], axis=1
    )


def flip(z, m):
    return sum(lax.rem(z // k + m // k % 2, 2) * k for k in (1, 2, 4))


def kernel(x_ref, w_hbm, ctx_hbm, pg, wg,
           w_ref, ctx_ref, g, qg, w_t, pt, wts, wto,
           bufa, sendb, recvb, sendc, recvc, y1, sendy, recvy, sendz, recvz,
           lsem, far_sem, gzs, gzr, gys, gyr,
           sa, ra, sb, rb, sc, rc, sd, rd, se, re, s1, r1, s2, r2, szs, szr):
    dp = lax.axis_index("dp")
    mp = lax.axis_index("mp")
    x, zh, c = dp // 4, lax.rem(dp // 2, 2), lax.rem(dp, 2)
    z, y = mp // NY, lax.rem(mp, NY)
    yp, ym, y2 = lax.rem(y + 1, NY), lax.rem(y + NY - 1, NY), lax.rem(y + 2, NY)
    depth = x_ref.shape[1]
    rows = x_ref.shape[0]
    half = depth // 2
    part = depth // (2 * Q)
    lo, hi = pl.ds(0, half), pl.ds(half, half)
    sib = (x * 4 + zh * 2 + (1 - c), mp)
    far = (x * 4 + (1 - zh) * 2 + c, mp)

    def xdev(k): return (lax.rem(x + k, NX) * 4 + zh * 2 + c, mp)
    def ydev(t): return (dp, z * NY + t)
    def zdev(m): return (dp, flip(z, m) * NY + y)
    def remote(src, dst, ss, rs, dev):
        return pltpu.make_async_remote_copy(src, dst, ss, rs, device_id=dev, device_id_type=MESH)

    own = pltpu.make_async_copy(x_ref, g.at[mp], lsem.at[0])
    load_w = pltpu.make_async_copy(w_hbm, w_ref, lsem.at[1])
    load_ctx = pltpu.make_async_copy(ctx_hbm, ctx_ref, lsem.at[2])
    own.start()
    load_w.start()
    load_ctx.start()
    def ring(k):
        t = lax.rem(zh * NZ + z + k + 2 * NZ, 2 * NZ)
        return (x * 4 + t // NZ * 2 + c, lax.rem(t, NZ) * NY + y)
    bar = pltpu.get_barrier_semaphore()
    relays = (ring(4), ring(-4))
    partners = (ydev(yp), ydev(ym), ydev(y2), ring(1), ring(-1), ring(2), ring(-2), sib, xdev(1), xdev(2), xdev(3), *relays)
    for dev in partners:
        pl.semaphore_signal(bar, inc=1, device_id=dev, device_id_type=MESH)
    pl.semaphore_wait(bar, len(partners))
    for dev in relays:
        pl.semaphore_signal(far_sem, inc=1, device_id=dev, device_id_type=MESH)
    own.wait()

    def ok(t): return jnp.logical_and(t >= 0, t < NZ)
    def when(cond, f, *args): pl.when(cond)(functools.partial(f, *args))
    def direct(d): return d >= DIRECT
    def zcopy(j, t, k):
        b = g.at[j * NY + y]
        return remote(b, b, gzs.at[j, k], gzr.at[j], (dp, t * NY + y))
    def ycopy(j, k):
        b = g.at[j * NY + (ym, yp)[k - 2], :, (lo, hi)[k - 2]] if k in (2, 3) else g.at[j * NY + y]
        return remote(b, b, gys.at[j, k], gyr.at[j, k], ydev((yp, ym, yp, ym, y2)[k]))
    def yarrive(j, k):
        b = g.at[j * NY + (ym, yp, y2, y2, y2)[k]]
        b = b.at[:, (lo, hi)[k - 2]] if k in (2, 3) else b
        return remote(b, b, gys.at[j, k], gyr.at[j, k], ydev(yp))
    def spread(j, d):
        for k in (4, 0, 1) if direct(d) else (0, 1):
            ycopy(j, k).start()
    def forward(j):
        yarrive(j, 0).wait_recv()
        ycopy(j, 2).start()
        yarrive(j, 1).wait_recv()
        ycopy(j, 3).start()
    def take(j, sg, d):
        zcopy(j, z, 0).wait_recv()
        if d % 2 == 0:
            for s in (1, 2):
                t = z - sg * s
                when(ok(t), lambda t, s: zcopy(j, t, s - 1).start(), t, s)
        spread(j, d)
    def complete(j, d):
        for k in (0, 1, 4) if direct(d) else (2, 3):
            yarrive(j, k).wait_recv()

    blocks = PATCHES // rows
    near = z // (NZ // 2)
    def image_back(image):
        first = pl.multiple_of(image * PATCHES, PATCHES)
        qkv = dot(g[pl.ds(image * blocks, blocks)].reshape(PATCHES, depth), w_ref[...], ((1,), (0,))).astype(BF16)
        qg[pl.ds(first, PATCHES), :] = attend(qkv, ctx_ref[pl.ds(first, PATCHES), :])

    sides = (-1, 1)
    for s in (1, 2):
        for i, sg in enumerate(sides):
            t = z + sg * s
            when(ok(t), lambda t, k: zcopy(z, t, k).start(), t, 2 * (s - 1) + i)
    spread(z, 0)
    load_w.wait()
    load_ctx.wait()
    w_t[...] = w_ref[...].T
    for d in range(1, NZ):
        for sg in sides:
            j = z + sg * d
            when(ok(j), take, j, sg, d)
        if not direct(d - 1):
            if d == 1:
                forward(z)
            else:
                for sg in sides:
                    j = z + sg * (d - 1)
                    when(ok(j), forward, j)
    if not direct(NZ - 1):
        for sg in sides:
            j = z + sg * (NZ - 1)
            when(ok(j), forward, j)
    def complete_all(ds, inside):
        for d in ds:
            for sg in sides if d else (1,):
                j = z + sg * d
                same = (j // (NZ // 2) == near) if inside else (j // (NZ // 2) != near)
                when(jnp.logical_and(ok(j), same), complete, j, d)
    complete_all(range(NZ // 2), True)
    image_back(near)
    complete_all(range(1, NZ), False)
    image_back(1 - near)

    tokens = g.shape[0] * rows
    def weight_term(h, q):
        cols = pl.ds(pl.multiple_of(h * half + q * part, HD), GROUP * part)
        return dot(g[:, :, cols].reshape(tokens, GROUP * part), qg[...], ((0,), (0,))).astype(BF16).reshape(GROUP, *wts.shape[1:])
    def cp_a(q): return remote(wts.at[q], bufa.at[q], sa.at[q], ra.at[q], sib)
    def cp_b(q, k): return remote(sendb.at[q, k - 1], recvb.at[q, k - 1], sb.at[q, k - 1], rb.at[q, k - 1], xdev(k))
    def cp_c(q): return remote(sendc.at[q], recvc.at[q], sc.at[q], rc.at[q], far)
    def cp_d(q, k):
        b = wg.at[c, q, x]
        return remote(b, b, sd.at[q, k - 1], rd.at[q, k - 1], xdev(k))
    def arr_d(q, k):
        b = wg.at[c, q, lax.rem(x + NX - k, NX)]
        return remote(b, b, sd.at[q, k - 1], rd.at[q, k - 1], sib)
    def cp_e(q): return remote(wg.at[c, q], wg.at[c, q], se.at[q], re.at[q], sib)
    def arr_e(q): return remote(wg.at[1 - c, q], wg.at[1 - c, q], se.at[q], re.at[q], sib)
    def stage_a(q):
        if q % GROUP == 0:
            wts[pl.ds(q, GROUP)] = weight_term(1 - c, q)
        cp_a(q).start()
    def stage_b(q):
        if q % GROUP == 0:
            wto[pl.ds(q, GROUP)] = weight_term(c, q)
        cp_a(q).wait_recv()
        for k in (2, 1, 3):
            p = lax.rem(x + k, NX)
            sendb[q, k - 1] = add(wto[q, p], bufa[q, p])
            cp_b(q, k).start()
    def stage_c(q):
        if q == 0:
            pl.semaphore_wait(far_sem, len(relays))
        for k in (1, 2, 3):
            cp_b(q, k).wait_recv()
        sendc[q] = add(wto[q, x], bufa[q, x], recvb[q, 0], recvb[q, 1], recvb[q, 2])
        cp_c(q).start()
    def stage_d(q):
        cp_c(q).wait_recv()
        wg[c, q, x] = add(sendc[q], recvc[q])
        for k in (2, 1, 3):
            cp_d(q, k).start()
    def stage_e(q):
        for k in (1, 2, 3):
            arr_d(q, k).wait_recv()
        cp_e(q).start()

    order = (7, 3, 5, 1, 6, 2, 4, 0)
    def cp_1(i, k):
        src = pt.at[i, y2, :, hi if k else lo]
        return remote(src, y1.at[i, k], s1.at[i, k], r1.at[i, k], ydev(ym if k else yp))
    def cp_2(i, k):
        return remote(sendy.at[i, k], recvy.at[i, k], s2.at[i, k], r2.at[i, k], ydev(ym if k else yp))
    def step_1(i):
        some = NY * rows
        first = pl.multiple_of(flip(z, order[i]) * some, some)
        pt[i] = dot(qg[pl.ds(first, some), :], w_t[...], ((1,), (0,))).astype(BF16).reshape(NY, rows, depth)
        cp_1(i, 0).start()
        cp_1(i, 1).start()
    def step_2(i):
        cp_1(i, 0).wait_recv()
        sendy[i, 0, :, lo] = add(pt[i, yp, :, lo], y1[i, 0])
        sendy[i, 0, :, hi] = pt[i, yp, :, hi]
        cp_2(i, 0).start()
        cp_1(i, 1).wait_recv()
        sendy[i, 1, :, lo] = pt[i, ym, :, lo]
        sendy[i, 1, :, hi] = add(pt[i, ym, :, hi], y1[i, 1])
        cp_2(i, 1).start()
    def cp_z(i):
        to, slot = ((1, i), (2, i), (4, 6))[(i >= 4) + (i >= 6)]
        return remote(sendz.at[i], recvz.at[slot], szs.at[slot], szr.at[slot], zdev(to))
    extra = {4: (0,), 5: (1,), 6: (2, 4), 7: (3, 5, 6)}
    def step_3(i):
        cp_2(i, 0).wait_recv()
        cp_2(i, 1).wait_recv()
        for slot in extra.get(i, ()):
            cp_z(slot).wait_recv()
        total = add(pt[i, y], recvy[i, 0], recvy[i, 1], *[recvz[slot] for slot in extra.get(i, ())])
        if i == NZ - 1:
            pg[...] = total
        else:
            sendz[i] = total
            cp_z(i).start()

    steps = []
    def at(t, f, i): steps.append((t, len(steps), f, i))
    for q in range(Q):
        at(T_A + 1.7 / Q * q, stage_a, q)
        at(T_B + B_STEP / Q * q, stage_b, q)
        at(T_C + B_STEP / Q * q, stage_c, q)
        at(T_D + D_STEP / Q * q, stage_d, q)
        at(T_E + D_STEP / Q * q, stage_e, q)
    for i in range(NZ):
        at(Y1 + Y_STEP * i, step_1, i)
        at(Y2 + Y_STEP * i, step_2, i)
        at(max(Y3 + Y_STEP * i, Z_AT[i]), step_3, i)
    for t, n, f, i in sorted(steps, key=lambda s: s[:2]):
        f(i)

    for q in range(Q):
        arr_e(q).wait_recv()
    for q in range(Q):
        cp_a(q).wait_send()
        cp_c(q).wait_send()
        cp_e(q).wait_send()
        for k in (1, 2, 3):
            cp_b(q, k).wait_send()
            cp_d(q, k).wait_send()
    for i in range(NZ):
        for k in (0, 1):
            cp_1(i, k).wait_send()
            cp_2(i, k).wait_send()
        if i < NZ - 1:
            cp_z(i).wait_send()
    for d in range(NZ):
        for sg in sides if d else (1,):
            j = z + sg * d
            def sent(j, sg, d):
                for k in (0, 1, 4) if direct(d) else range(4):
                    ycopy(j, k).wait_send()
                if d and d % 2 == 0:
                    for s in (1, 2):
                        when(ok(z - sg * s), lambda s: zcopy(j, z, s - 1).wait_send(), s)
            when(ok(j), sent, j, sg, d)
    for s in (1, 2):
        for i, sg in enumerate(sides):
            when(ok(z + sg * s), lambda k: zcopy(z, z, k).wait_send(), 2 * (s - 1) + i)


def per_device(patches, qkv_weight, context_grad):
    rows, depth = patches.shape
    cols = qkv_weight.shape[1]
    R = depth // (2 * Q * NX)
    D, S = pltpu.SemaphoreType.DMA, pltpu.VMEM
    def buf(*shape): return S(shape, BF16)
    pg, wg = pl.pallas_call(
        kernel,
        out_shape=[jax.ShapeDtypeStruct((rows, depth), BF16), jax.ShapeDtypeStruct((2, Q, NX, R, cols), BF16)],
        in_specs=[pl.BlockSpec(memory_space=pltpu.HBM)] * 3,
        out_specs=[pl.BlockSpec(memory_space=pltpu.VMEM)] * 2,
        scratch_shapes=[
            buf(depth, cols), buf(*context_grad.shape), buf(NZ * NY, rows, depth), buf(NZ * NY * rows, cols), buf(cols, depth), buf(NZ, NY, rows, depth),
            buf(Q, NX, R, cols), buf(Q, NX, R, cols),
            buf(Q, NX, R, cols), buf(Q, 3, R, cols), buf(Q, 3, R, cols), buf(Q, R, cols), buf(Q, R, cols),
            buf(NZ, 2, rows, depth // 2), buf(NZ, 2, rows, depth), buf(NZ, 2, rows, depth),
            buf(NZ - 1, rows, depth), buf(NZ - 1, rows, depth),
            D((3,)), pltpu.SemaphoreType.REGULAR, D((NZ, 4)), D((NZ,)), D((NZ, 5)), D((NZ, 5)),
            D((Q,)), D((Q,)), D((Q, 3)), D((Q, 3)), D((Q,)), D((Q,)), D((Q, 3)), D((Q, 3)), D((Q,)), D((Q,)),
            D((NZ, 2)), D((NZ, 2)), D((NZ, 2)), D((NZ, 2)), D((NZ - 1,)), D((NZ - 1,)),
        ],
        compiler_params=pltpu.CompilerParams(collective_id=1, has_side_effects=True, vmem_limit_bytes=50 << 20),
        name="attention_back",
    )(patches, qkv_weight, context_grad)
    return pg, wg.reshape(depth, cols)


def solution(mesh):
    in_specs = (P(("dp", "mp"), None), P(None, "mp"), P("dp", "mp"))
    out_specs = (P(("dp", "mp"), None), P(None, "mp"))
    return jax.shard_map(
        per_device, mesh=mesh, in_specs=in_specs, out_specs=out_specs, check_vma=False
    )
```

```python
import functools
import jax
import jax.numpy as jnp
from jax import lax
from jax.experimental import pallas as pl
from jax.experimental.pallas import tpu as pltpu
from jax.sharding import PartitionSpec as P

MESH = pl.DeviceIdType.MESH
NZ, NY, NX = 8, 4, 4
HD = 128
PATCHES = 256
Q, GROUP = 6, 1
DIRECT = 6
T_A, T_B, T_C, T_D, T_E = 0.0, 3.5, 8.5, 28.0, 33.0
B_STEP, D_STEP = 12.4, 28.0
Y1, Y2, Y3, Y_STEP = 1.0, 5.0, 10.0, 2.7
Z_AT = (0, 0, 0, 0, 24, 27, 33, 60)
F32, BF16 = jnp.float32, jnp.bfloat16


def add(*terms):
    total = terms[0].astype(F32)
    for t in terms[1:]:
        total = total + t.astype(F32)
    return total.astype(BF16)


def dot(a, b, dims):
    return lax.dot_general(a, b, (dims, ((), ())), preferred_element_type=F32)


def normalize(t):
    t = t.astype(F32)
    centred = t - jnp.mean(t, axis=-1, keepdims=True)
    r = lax.rsqrt(jnp.mean(centred * centred, axis=-1, keepdims=True) + 1e-06)
    return centred * r, r


def norm_back(g, n, r):
    return (g - jnp.mean(g, axis=-1, keepdims=True) - n * jnp.mean(g * n, axis=-1, keepdims=True)) * r


def attend(qkv, ctx):
    qn, qr = normalize(qkv[:, :HD])
    kn, kr = normalize(qkv[:, HD : 2 * HD])
    v = qkv[:, 2 * HD :]
    qb, kb = qn.astype(BF16), kn.astype(BF16)
    f = 1.0 / HD**0.5
    ex = jnp.exp(dot(kb, qb, ((1,), (1,))) * f)
    p = ex / jnp.sum(ex, axis=0, keepdims=True)
    dsoft = dot(v, ctx, ((1,), (1,)))
    delta = jnp.sum(p * dsoft, axis=0, keepdims=True)
    ds = (p * (dsoft - delta) * f).astype(BF16)
    dv = dot(p.astype(BF16), ctx, ((1,), (0,)))
    dkn = dot(ds, qb, ((1,), (0,)))
    dqn = dot(ds, kb, ((0,), (0,)))
    return jnp.concatenate(
        [norm_back(dqn, qn, qr).astype(BF16), norm_back(dkn, kn, kr).astype(BF16), dv.astype(BF16)], axis=1
    )


def flip(z, m):
    return sum(lax.rem(z // k + m // k % 2, 2) * k for k in (1, 2, 4))


def kernel(x_ref, w_hbm, ctx_hbm, pg, wg,
           w_ref, ctx_ref, g, qg, w_t, pt, wts, wto,
           bufa, sendb, recvb, sendc, recvc, y1, sendy, recvy, sendz, recvz,
           lsem, far_sem, gzs, gzr, gys, gyr,
           sa, ra, sb, rb, sc, rc, sd, rd, se, re, s1, r1, s2, r2, szs, szr):
    dp = lax.axis_index("dp")
    mp = lax.axis_index("mp")
    x, zh, c = dp // 4, lax.rem(dp // 2, 2), lax.rem(dp, 2)
    z, y = mp // NY, lax.rem(mp, NY)
    yp, ym, y2 = lax.rem(y + 1, NY), lax.rem(y + NY - 1, NY), lax.rem(y + 2, NY)
    depth = x_ref.shape[1]
    rows = x_ref.shape[0]
    half = depth // 2
    part = depth // (2 * Q)
    lo, hi = pl.ds(0, half), pl.ds(half, half)
    sib = (x * 4 + zh * 2 + (1 - c), mp)
    far = (x * 4 + (1 - zh) * 2 + c, mp)

    def xdev(k): return (lax.rem(x + k, NX) * 4 + zh * 2 + c, mp)
    def ydev(t): return (dp, z * NY + t)
    def zdev(m): return (dp, flip(z, m) * NY + y)
    def remote(src, dst, ss, rs, dev):
        return pltpu.make_async_remote_copy(src, dst, ss, rs, device_id=dev, device_id_type=MESH)

    own = pltpu.make_async_copy(x_ref, g.at[mp], lsem.at[0])
    load_w = pltpu.make_async_copy(w_hbm, w_ref, lsem.at[1])
    load_ctx = pltpu.make_async_copy(ctx_hbm, ctx_ref, lsem.at[2])
    own.start()
    load_w.start()
    load_ctx.start()
    def ring(k):
        t = lax.rem(zh * NZ + z + k + 2 * NZ, 2 * NZ)
        return (x * 4 + t // NZ * 2 + c, lax.rem(t, NZ) * NY + y)
    bar = pltpu.get_barrier_semaphore()
    relays = (ring(4), ring(-4))
    partners = (ydev(yp), ydev(ym), ydev(y2), ring(1), ring(-1), ring(2), ring(-2), sib, xdev(1), xdev(2), xdev(3), *relays)
    for dev in partners:
        pl.semaphore_signal(bar, inc=1, device_id=dev, device_id_type=MESH)
    pl.semaphore_wait(bar, len(partners))
    for dev in relays:
        pl.semaphore_signal(far_sem, inc=1, device_id=dev, device_id_type=MESH)
    own.wait()

    def ok(t): return jnp.logical_and(t >= 0, t < NZ)
    def when(cond, f, *args): pl.when(cond)(functools.partial(f, *args))
    def direct(d): return d >= DIRECT
    def zcopy(j, t, k):
        b = g.at[j * NY + y]
        return remote(b, b, gzs.at[j, k], gzr.at[j], (dp, t * NY + y))
    def ycopy(j, k):
        b = g.at[j * NY + (ym, yp)[k - 2], :, (lo, hi)[k - 2]] if k in (2, 3) else g.at[j * NY + y]
        return remote(b, b, gys.at[j, k], gyr.at[j, k], ydev((yp, ym, yp, ym, y2)[k]))
    def yarrive(j, k):
        b = g.at[j * NY + (ym, yp, y2, y2, y2)[k]]
        b = b.at[:, (lo, hi)[k - 2]] if k in (2, 3) else b
        return remote(b, b, gys.at[j, k], gyr.at[j, k], ydev(yp))
    def spread(j, d):
        for k in (4, 0, 1) if direct(d) else (0, 1):
            ycopy(j, k).start()
    def forward(j):
        yarrive(j, 0).wait_recv()
        ycopy(j, 2).start()
        yarrive(j, 1).wait_recv()
        ycopy(j, 3).start()
    def take(j, sg, d):
        zcopy(j, z, 0).wait_recv()
        if d % 2 == 0:
            for s in (1, 2):
                t = z - sg * s
                when(ok(t), lambda t, s: zcopy(j, t, s - 1).start(), t, s)
        spread(j, d)
    def complete(j, d):
        for k in (0, 1, 4) if direct(d) else (2, 3):
            yarrive(j, k).wait_recv()

    blocks = PATCHES // rows
    near = z // (NZ // 2)
    def image_back(image):
        first = pl.multiple_of(image * PATCHES, PATCHES)
        qkv = dot(g[pl.ds(image * blocks, blocks)].reshape(PATCHES, depth), w_ref[...], ((1,), (0,))).astype(BF16)
        qg[pl.ds(first, PATCHES), :] = attend(qkv, ctx_ref[pl.ds(first, PATCHES), :])

    sides = (-1, 1)
    for s in (1, 2):
        for i, sg in enumerate(sides):
            t = z + sg * s
            when(ok(t), lambda t, k: zcopy(z, t, k).start(), t, 2 * (s - 1) + i)
    spread(z, 0)
    load_w.wait()
    load_ctx.wait()
    w_t[...] = w_ref[...].T
    for d in range(1, NZ):
        for sg in sides:
            j = z + sg * d
            when(ok(j), take, j, sg, d)
        if not direct(d - 1):
            if d == 1:
                forward(z)
            else:
                for sg in sides:
                    j = z + sg * (d - 1)
                    when(ok(j), forward, j)
    if not direct(NZ - 1):
        for sg in sides:
            j = z + sg * (NZ - 1)
            when(ok(j), forward, j)
    def complete_all(ds, inside):
        for d in ds:
            for sg in sides if d else (1,):
                j = z + sg * d
                same = (j // (NZ // 2) == near) if inside else (j // (NZ // 2) != near)
                when(jnp.logical_and(ok(j), same), complete, j, d)
    complete_all(range(NZ // 2), True)
    image_back(near)
    complete_all(range(1, NZ), False)
    image_back(1 - near)

    tokens = g.shape[0] * rows
    def weight_term(h, q):
        cols = pl.ds(pl.multiple_of(h * half + q * part, HD), GROUP * part)
        return dot(g[:, :, cols].reshape(tokens, GROUP * part), qg[...], ((0,), (0,))).astype(BF16).reshape(GROUP, *wts.shape[1:])
    def cp_a(q): return remote(wts.at[q], bufa.at[q], sa.at[q], ra.at[q], sib)
    def cp_b(q, k): return remote(sendb.at[q, k - 1], recvb.at[q, k - 1], sb.at[q, k - 1], rb.at[q, k - 1], xdev(k))
    def cp_c(q): return remote(sendc.at[q], recvc.at[q], sc.at[q], rc.at[q], far)
    def cp_d(q, k):
        b = wg.at[c, q, x]
        return remote(b, b, sd.at[q, k - 1], rd.at[q, k - 1], xdev(k))
    def arr_d(q, k):
        b = wg.at[c, q, lax.rem(x + NX - k, NX)]
        return remote(b, b, sd.at[q, k - 1], rd.at[q, k - 1], sib)
    def cp_e(q): return remote(wg.at[c, q], wg.at[c, q], se.at[q], re.at[q], sib)
    def arr_e(q): return remote(wg.at[1 - c, q], wg.at[1 - c, q], se.at[q], re.at[q], sib)
    def stage_a(q):
        if q % GROUP == 0:
            wts[pl.ds(q, GROUP)] = weight_term(1 - c, q)
        cp_a(q).start()
    def stage_b(q):
        if q % GROUP == 0:
            wto[pl.ds(q, GROUP)] = weight_term(c, q)
        cp_a(q).wait_recv()
        for k in (2, 1, 3):
            p = lax.rem(x + k, NX)
            sendb[q, k - 1] = add(wto[q, p], bufa[q, p])
            cp_b(q, k).start()
    def stage_c(q):
        if q == 0:
            pl.semaphore_wait(far_sem, len(relays))
        for k in (1, 2, 3):
            cp_b(q, k).wait_recv()
        sendc[q] = add(wto[q, x], bufa[q, x], recvb[q, 0], recvb[q, 1], recvb[q, 2])
        cp_c(q).start()
    def stage_d(q):
        cp_c(q).wait_recv()
        wg[c, q, x] = add(sendc[q], recvc[q])
        for k in (2, 1, 3):
            cp_d(q, k).start()
    def stage_e(q):
        for k in (1, 2, 3):
            arr_d(q, k).wait_recv()
        cp_e(q).start()

    order = (7, 3, 5, 1, 6, 2, 4, 0)
    def cp_1(i, k):
        src = pt.at[i, y2, :, hi if k else lo]
        return remote(src, y1.at[i, k], s1.at[i, k], r1.at[i, k], ydev(ym if k else yp))
    def cp_2(i, k):
        return remote(sendy.at[i, k], recvy.at[i, k], s2.at[i, k], r2.at[i, k], ydev(ym if k else yp))
    def step_1(i):
        some = NY * rows
        first = pl.multiple_of(flip(z, order[i]) * some, some)
        pt[i] = dot(qg[pl.ds(first, some), :], w_t[...], ((1,), (0,))).astype(BF16).reshape(NY, rows, depth)
        cp_1(i, 0).start()
        cp_1(i, 1).start()
    def step_2(i):
        cp_1(i, 0).wait_recv()
        sendy[i, 0, :, lo] = add(pt[i, yp, :, lo], y1[i, 0])
        sendy[i, 0, :, hi] = pt[i, yp, :, hi]
        cp_2(i, 0).start()
        cp_1(i, 1).wait_recv()
        sendy[i, 1, :, lo] = pt[i, ym, :, lo]
        sendy[i, 1, :, hi] = add(pt[i, ym, :, hi], y1[i, 1])
        cp_2(i, 1).start()
    def cp_z(i):
        to, slot = ((1, i), (2, i), (4, 6))[(i >= 4) + (i >= 6)]
        return remote(sendz.at[i], recvz.at[slot], szs.at[slot], szr.at[slot], zdev(to))
    extra = {4: (0,), 5: (1,), 6: (2, 4), 7: (3, 5, 6)}
    def step_3(i):
        cp_2(i, 0).wait_recv()
        cp_2(i, 1).wait_recv()
        for slot in extra.get(i, ()):
            cp_z(slot).wait_recv()
        total = add(pt[i, y], recvy[i, 0], recvy[i, 1], *[recvz[slot] for slot in extra.get(i, ())])
        if i == NZ - 1:
            pg[...] = total
        else:
            sendz[i] = total
            cp_z(i).start()

    steps = []
    def at(t, f, i): steps.append((t, len(steps), f, i))
    for q in range(Q):
        at(T_A + 1.7 / Q * q, stage_a, q)
        at(T_B + B_STEP / Q * q, stage_b, q)
        at(T_C + B_STEP / Q * q, stage_c, q)
        at(T_D + D_STEP / Q * q, stage_d, q)
        at(T_E + D_STEP / Q * q, stage_e, q)
    for i in range(NZ):
        at(Y1 + Y_STEP * i, step_1, i)
        at(Y2 + Y_STEP * i, step_2, i)
        at(max(Y3 + Y_STEP * i, Z_AT[i]), step_3, i)
    for t, n, f, i in sorted(steps, key=lambda s: s[:2]):
        f(i)

    for q in range(Q):
        arr_e(q).wait_recv()
    for q in range(Q):
        cp_a(q).wait_send()
        cp_c(q).wait_send()
        cp_e(q).wait_send()
        for k in (1, 2, 3):
            cp_b(q, k).wait_send()
            cp_d(q, k).wait_send()
    for i in range(NZ):
        for k in (0, 1):
            cp_1(i, k).wait_send()
            cp_2(i, k).wait_send()
        if i < NZ - 1:
            cp_z(i).wait_send()
    for d in range(NZ):
        for sg in sides if d else (1,):
            j = z + sg * d
            def sent(j, sg, d):
                for k in (0, 1, 4) if direct(d) else range(4):
                    ycopy(j, k).wait_send()
                if d and d % 2 == 0:
                    for s in (1, 2):
                        when(ok(z - sg * s), lambda s: zcopy(j, z, s - 1).wait_send(), s)
            when(ok(j), sent, j, sg, d)
    for s in (1, 2):
        for i, sg in enumerate(sides):
            when(ok(z + sg * s), lambda k: zcopy(z, z, k).wait_send(), 2 * (s - 1) + i)


def per_device(patches, qkv_weight, context_grad):
    rows, depth = patches.shape
    cols = qkv_weight.shape[1]
    R = depth // (2 * Q * NX)
    D, S = pltpu.SemaphoreType.DMA, pltpu.VMEM
    def buf(*shape): return S(shape, BF16)
    pg, wg = pl.pallas_call(
        kernel,
        out_shape=[jax.ShapeDtypeStruct((rows, depth), BF16), jax.ShapeDtypeStruct((2, Q, NX, R, cols), BF16)],
        in_specs=[pl.BlockSpec(memory_space=pltpu.HBM)] * 3,
        out_specs=[pl.BlockSpec(memory_space=pltpu.VMEM)] * 2,
        scratch_shapes=[
            buf(depth, cols), buf(*context_grad.shape), buf(NZ * NY, rows, depth), buf(NZ * NY * rows, cols), buf(cols, depth), buf(NZ, NY, rows, depth),
            buf(Q, NX, R, cols), buf(Q, NX, R, cols),
            buf(Q, NX, R, cols), buf(Q, 3, R, cols), buf(Q, 3, R, cols), buf(Q, R, cols), buf(Q, R, cols),
            buf(NZ, 2, rows, depth // 2), buf(NZ, 2, rows, depth), buf(NZ, 2, rows, depth),
            buf(NZ - 1, rows, depth), buf(NZ - 1, rows, depth),
            D((3,)), pltpu.SemaphoreType.REGULAR, D((NZ, 4)), D((NZ,)), D((NZ, 5)), D((NZ, 5)),
            D((Q,)), D((Q,)), D((Q, 3)), D((Q, 3)), D((Q,)), D((Q,)), D((Q, 3)), D((Q, 3)), D((Q,)), D((Q,)),
            D((NZ, 2)), D((NZ, 2)), D((NZ, 2)), D((NZ, 2)), D((NZ - 1,)), D((NZ - 1,)),
        ],
        compiler_params=pltpu.CompilerParams(collective_id=1, has_side_effects=True, vmem_limit_bytes=50 << 20),
        name="attention_back",
    )(patches, qkv_weight, context_grad)
    return pg, wg.reshape(depth, cols)


def solution(mesh):
    in_specs = (P(("dp", "mp"), None), P(None, "mp"), P("dp", "mp"))
    out_specs = (P(("dp", "mp"), None), P(None, "mp"))
    return jax.shard_map(
        per_device, mesh=mesh, in_specs=in_specs, out_specs=out_specs, check_vma=False
    )
```
